32 devices in a mesh: beam: 4 (over y, x), chan: 8 (over z, core).
Axes of the slice: x: 2, y: 2, z: 4, core: 2. Of those that a mesh axis runs over, the one named last changes fastest.
Arguments:
- intensities: bfloat16 [32, 8192, 128], P(None, ('beam', 'chan')), may hold values from -6 to 6
- lower_index: int32 [10, 1024], replicated, may hold values from 0 to 511, as said below
- upper_index: int32 [10, 1024], replicated, may hold values from 0 to 511, as said below
- delay_shift: int32 [10, 1024], replicated, may hold values from 0 to 512, as said below
- widths: int32 [8], replicated, may hold values from 1 to 64, as said below
- max_delay: int32 [32], P(('beam', 'chan')), may hold values from 256 to 1023
Outputs:
- snr: float32 [32, 8, 1024], P(('beam', 'chan'))
The draws below stay inside these ranges and needn't reach their ends.
Inputs may be any that keep to these rules, and one draw needn't show every extreme that they name: `lower_index`: at level l and row r, with d = r mod 2^(l+1), the entry is either floor(d / 2) or min(floor((d + 1) / 2), 2^l - 1). `upper_index`: at level l and row r, with d = r mod 2^(l+1), the entry is either floor(d / 2) or min(floor((d + 1) / 2), 2^l - 1). `delay_shift`: at level l the shift is at most 2^l. Distinct widths; 1 and 64 are always among them.
All inputs are finite; a program needn't handle non-finite values.
Results may differ from the reference program's by a relative error of at most 0.0003.
Values sent between devices are 32-bit elements; how exact they have to be, the bound alone decides.
A program may use at most 64 MiB of HBM per device.

```python
import jax
import jax.numpy as jnp
from jax import lax

C = 8192
DM_LOG = 10
DM_TOP = 1024
SUB0 = 8
SAMPLES = 128
BEAMS = 32
NBOX = 8
MAXW = 64


def fdmt_tables(key):
    level_ids = jnp.arange(DM_LOG, dtype=jnp.int32)[:, None]
    row_ids = jnp.arange(DM_TOP, dtype=jnp.int32)[None, :]
    rows_now = jnp.left_shift(jnp.int32(1), level_ids + 1)
    rows_before = rows_now // 2
    trial = row_ids % rows_now
    coin = jax.random.randint(jax.random.fold_in(key, 11), (DM_LOG, DM_TOP), 0, 2, dtype=jnp.int32)
    lower_part = jnp.minimum((trial + coin) // 2, rows_before - 1)
    upper_part = jnp.minimum(trial - lower_part, rows_before - 1)
    moved = lower_part + trial % 2
    return (lower_part.astype(jnp.int32), upper_part.astype(jnp.int32), moved.astype(jnp.int32))


def draw_lower_index(key, part):
    return fdmt_tables(key)[0]


def draw_upper_index(key, part):
    return fdmt_tables(key)[1]


def draw_delay_shift(key, part):
    return fdmt_tables(key)[2]


def draw_widths(key, part):
    inner = jax.random.permutation(jax.random.fold_in(key, 5), MAXW - 2)[:NBOX - 2] + 2
    values = jnp.concatenate([jnp.array([1, MAXW], dtype=jnp.int32), inner.astype(jnp.int32)])
    order = jax.random.permutation(jax.random.fold_in(key, 6), NBOX)
    return values[order].astype(jnp.int32)


def draw_max_delay(key, part):
    values = jax.random.randint(jax.random.fold_in(key, 21), (BEAMS,), DM_TOP // 4, DM_TOP, dtype=jnp.int32)
    first_pick = jax.random.randint(jax.random.fold_in(key, 22), (), 0, BEAMS, dtype=jnp.int32)
    second_pick = (first_pick + 1 + jax.random.randint(jax.random.fold_in(key, 23), (), 0, BEAMS - 1, dtype=jnp.int32)) % BEAMS
    places = jnp.arange(BEAMS, dtype=jnp.int32)
    values = jnp.where(places == first_pick, DM_TOP - 1, values)
    values = jnp.where(places == second_pick, DM_TOP // 4, values)
    return values.astype(jnp.int32)


def levels(rng, extent, split, least, largest):
    gain = 1.0
    for dim, shards_of in split:
        heights = jax.random.uniform(jax.random.fold_in(jax.random.fold_in(rng, 6), dim), (shards_of,), jnp.float32, least / len(split), largest / len(split))
        gain = gain * jnp.repeat(jnp.exp(heights), extent[dim] // shards_of).reshape((-1,) + (1,) * (len(extent) - 1 - dim))
    return gain


def noise(key, shape, deviation, most, shards=(), kind=jnp.bfloat16):
    values = jax.random.normal(key, shape, jnp.float32) * deviation
    if len(shards) > 0:
        values = levels(key, shape, shards, -0.22, 0.18) * values
    return jnp.clip(values, min=-most, max=most).astype(kind)


def setup_inputs(seed: int = 0) -> dict:
    keys = jax.random.split(jax.random.key(seed), 7)
    intensities = noise(keys[0], (BEAMS, C, SAMPLES), 1.0, 6.0, ((1, 32),))
    lower_index = draw_lower_index(jax.random.fold_in(keys[6], 71), 0)
    upper_index = draw_upper_index(jax.random.fold_in(keys[6], 71), 0)
    delay_shift = draw_delay_shift(jax.random.fold_in(keys[6], 71), 0)
    widths = draw_widths(jax.random.fold_in(keys[6], 71), 0)
    max_delay = draw_max_delay(jax.random.fold_in(keys[6], 71), 0)
    return {"intensities": intensities, "lower_index": lower_index, "upper_index": upper_index, "delay_shift": delay_shift, "widths": widths, "max_delay": max_delay}


def delayed(values, amounts):
    samples_here = values.shape[-1]
    time_index = jnp.arange(samples_here, dtype=jnp.int32)
    source = time_index[None, None, :] - amounts[..., None]
    fetched = jnp.take_along_axis(values, jnp.maximum(source, 0).astype(jnp.int32), axis=-1)
    return jnp.where(source >= 0, fetched, jnp.zeros_like(fetched))

def pick_rows(state_part, index_table):
    return jax.vmap(lambda block_in, index_in: jnp.take(block_in, index_in, axis=0))(state_part, index_table)

def fdmt_beam(block, lower_index, upper_index, delay_shift):
    state = lax.optimization_barrier(jnp.sum(block.reshape(DM_TOP, SUB0, SAMPLES), axis=1, dtype=jnp.float32))[:, None, :]
    for merge_step in range(DM_LOG):
        pair_count = state.shape[0] // 2
        new_rows = 2 * state.shape[1]
        lower_table = lower_index[merge_step].reshape(pair_count, new_rows)
        upper_table = upper_index[merge_step].reshape(pair_count, new_rows)
        shift_table = delay_shift[merge_step].reshape(pair_count, new_rows)
        lower_rows = pick_rows(state[0::2], lower_table)
        upper_rows = pick_rows(state[1::2], upper_table)
        state = lower_rows + delayed(upper_rows, shift_table)
    return state[0]

def scores(trials, widths, limit):
    running = jnp.cumsum(trials, axis=-1)
    padded = jnp.concatenate([jnp.zeros((DM_TOP, MAXW), running.dtype), running], axis=-1)

    def one_width(width):
        earlier = lax.dynamic_slice_in_dim(padded, (MAXW - width).astype(jnp.int32), SAMPLES, axis=1)
        boxcar = running - earlier
        center = lax.optimization_barrier(jnp.mean(boxcar, axis=-1, keepdims=True))
        offset = boxcar - center
        spread = lax.optimization_barrier(jnp.mean(offset * offset, axis=-1, keepdims=True))
        return lax.optimization_barrier(jnp.max(offset / jnp.sqrt(spread + 1e-05), axis=-1))
    table = lax.map(one_width, widths)
    keep_rows = jnp.arange(DM_TOP, dtype=jnp.int32) <= limit
    return jnp.where(keep_rows[None, :], table, jnp.zeros_like(table))

def reference(intensities, lower_index, upper_index, delay_shift, widths, max_delay):

    def one_beam(packed):
        block, limit = packed
        trials = fdmt_beam(block, lower_index, upper_index, delay_shift)
        return scores(trials, widths, limit)
    return lax.map(one_beam, (intensities, max_delay))
```

```python
import functools

import jax
import jax.numpy as jnp
from jax import lax
from jax.experimental import pallas as pl
from jax.experimental.pallas import tpu as pltpu
from jax.sharding import PartitionSpec as P

SUB0 = 8
ROWS = 8
BATCH = 16
MESH = pl.DeviceIdType.MESH


def take(values, index, axis):
    return jnp.take_along_axis(values, index, axis=axis, mode="promise_in_bounds")


def source_base(trial, width):
    half = width // 2
    return jnp.minimum(4 * (trial // ROWS), jnp.maximum(half - ROWS, 0))


def build_indices(steps, lower, upper, shift, low_at, up_at, time_at, samples):
    levels, bands = lower.shape
    kept = low_at.shape[1]
    depth = 16
    zeros = jnp.zeros((depth - levels, bands), jnp.int32)
    lower = jnp.concatenate([lower, zeros], axis=0)
    upper = jnp.concatenate([upper, zeros], axis=0)
    shift = jnp.concatenate([shift, zeros], axis=0)
    level = lax.broadcasted_iota(jnp.int32, (depth, bands), 0)
    row = lax.broadcasted_iota(jnp.int32, (depth, bands), 1)
    width = jnp.left_shift(jnp.int32(2), level)
    trial = row & (width - 1)
    inside = (row & (ROWS - 1)) - trial
    skip = source_base(trial, width)
    lower = jnp.where(level <= 2, inside + lower, lower - skip) & (ROWS - 1)
    upper = jnp.where(level <= 2, inside + width // 2 + upper, upper - skip) & (ROWS - 1)
    packed = jnp.concatenate(
        [(lower + ROWS * upper).astype(jnp.float32), jnp.minimum(shift, samples).astype(jnp.float32)],
        axis=0,
    ).astype(jnp.bfloat16)
    entry = lax.broadcasted_iota(jnp.int32, (2 * depth, samples), 0)
    time = lax.broadcasted_iota(jnp.int32, (kept, samples), 1)
    for at, step in enumerate(steps):
        spread = jnp.where(entry == step, 256.0, jnp.where(entry == depth + step, 1.0, 0.0))
        value = lax.dot_general(
            packed,
            spread.astype(jnp.bfloat16),
            (((0,), (0,)), ((), ())),
            preferred_element_type=jnp.float32,
        )[:kept].astype(jnp.int32)
        low_at[at] = (value >> 8) & (ROWS - 1)
        up_at[at] = value >> 11
        time_at[at] = time - (value & 255)


def merge(lowers, uppers, lows, ups, whens, samples):
    uppers = [take(v, up, 0) for v, up in zip(uppers, ups)]
    lowers = [take(v, low, 0) for v, low in zip(lowers, lows)]
    uppers = [take(v, when & (samples - 1), 1) for v, when in zip(uppers, whens)]
    return [v + jnp.where(when >= 0, u, 0.0) for v, u, when in zip(lowers, uppers, whens)]


def places_of(step, start, size, first, last):
    width = 2 << step
    places = []
    for base in range(0, size, width):
        for trial in range(first, last, ROWS):
            skip = min(4 * (trial // ROWS), max(width // 2 - ROWS, 0))
            places.append((base + trial, start + base + trial, start + base + skip, start + base + width // 2 + skip))
    return places


def scores(trials_ref, start, size, widths_ref, limit_ref, out_ref, samples):
    boxes = out_ref.shape[1]
    chunk = min(256, size)
    source = lax.broadcasted_iota(jnp.int32, (samples, 2 * samples), 1) % samples
    target = lax.broadcasted_iota(jnp.int32, (samples, 2 * samples), 0)
    limit = limit_ref[0]
    kernels = []
    for box in range(boxes):
        width = widths_ref[box]
        back = target - source
        hit = jnp.where((back >= 0) & (back < width), 1.0, 0.0)
        mean = jnp.minimum(width, samples - source).astype(jnp.float32) * (1.0 / samples)
        kernels.append((hit - mean).astype(jnp.bfloat16))
    for at in range(start, start + size, chunk):
        trials = trials_ref[pl.ds(at, chunk)]
        high = trials.astype(jnp.bfloat16)
        low = (trials - high.astype(jnp.float32)).astype(jnp.bfloat16)
        both = jnp.concatenate([high, low], axis=1)
        keep = lax.broadcasted_iota(jnp.int32, (1, chunk), 1) + at <= limit
        for box in range(boxes):
            offset = lax.dot_general(
                kernels[box], both, (((1,), (1,)), ((), ())), preferred_element_type=jnp.float32
            )
            top = jnp.max(offset, axis=0, keepdims=True)
            spread = jnp.sum(offset * offset, axis=0, keepdims=True) * (1.0 / samples)
            value = jnp.where(keep, top / jnp.sqrt(spread + 1e-05), 0.0)
            out_ref[0, pl.ds(box, 1), pl.ds(at, chunk)] = value


def kernel(
    beam_count, chan_count, levels, pieces,
    x_hbm, lower_hbm, upper_hbm, shift_hbm, widths_hbm, limit_hbm, out_ref,
    x_ref, lower_ref, upper_ref, shift_ref, widths_ref, limit_ref, work, ready, got, *rest,
):
    count = beam_count * chan_count
    channels, samples = x_ref.shape[1], x_ref.shape[2]
    rows_each = channels // SUB0
    bands = count * rows_each
    local = rows_each.bit_length() - 1
    states, rest = rest[: levels - local], rest[levels - local :]
    low_in, up_in, time_in, low_at, up_at, time_at, load_sem, table_sem, send_sem, recv_sem = rest
    beam, chan = lax.axis_index("beam"), lax.axis_index("chan")
    me = beam * chan_count + chan
    piece_rows = rows_each // pieces

    pair, core = chan // 2, chan % 2
    half = chan_count // 4
    side = pair // half
    far = [(1 - side) * half + at for at in range(half)]
    near = [side * half + (pair + 1 + at) % half for at in range(half)]
    beam_steps = [(1 << bit) * (1 - 2 * (beam // (1 << bit) % 2)) for bit in range(beam_count.bit_length() - 1)]

    def other_beam(mask):
        value = beam
        for bit, step in enumerate(beam_steps):
            if mask >> bit & 1:
                value = value + step
        return value

    def group(pair_to):
        return [(other_beam(mask), pair_to * 2 + (core + turn) % 2) for mask in range(beam_count) for turn in range(2)]

    order = [(pair_to, group(pair_to)) for pair_to in far[:1] + near + far[1:]]
    own = half

    barrier = pltpu.get_barrier_semaphore()
    others = [(lower_hbm, lower_ref), (upper_hbm, upper_ref), (shift_hbm, shift_ref), (widths_hbm, widths_ref), (limit_hbm, limit_ref)]
    tables = [pltpu.make_async_copy(source, target, table_sem.at[at]) for at, (source, target) in enumerate(others)]
    for table in tables:
        table.start()
    loads = []
    for at, (pair_to, _) in enumerate(order):
        loads.append([])
        for mask in range(beam_count):
            rows = pl.ds(other_beam(mask) * chan_count + pair_to * 2, 2)
            load = pltpu.make_async_copy(x_hbm.at[rows], x_ref.at[rows], load_sem.at[at, mask])
            load.start()
            loads[-1].append(load)
    for at, (_, devices) in enumerate(order):
        for place, device in enumerate(devices):
            if (at, place) != (own, 0):
                pl.semaphore_signal(barrier, inc=1, device_id=device, device_id_type=MESH)

    band = lax.broadcasted_iota(jnp.int32, (rows_each, channels), 0)
    channel = lax.broadcasted_iota(jnp.int32, (rows_each, channels), 1)
    adder = jnp.where(channel // SUB0 == band, 1.0, 0.0).astype(jnp.bfloat16)
    for table in tables:
        table.wait()
    block = 128
    first = me * rows_each
    lanes = pl.ds(pl.multiple_of(first // block * block, block), block)
    away = (block - first % block) % block
    mine = [pltpu.roll(ref[:, lanes], away, 1) for ref in (lower_ref, upper_ref, shift_ref)]
    build_indices(range(local), *mine, low_in, up_in, time_in, samples)

    def dedisperse(beams):
        sums = [jnp.dot(adder, x_ref[at], preferred_element_type=jnp.float32) for at in beams]
        tiles = [(at, row) for at in beams for row in range(0, rows_each, ROWS)]
        values = [v[row : row + ROWS] for v in sums for row in range(0, rows_each, ROWS)]
        for step in range(local):
            lows = [low_in[step, pl.ds(row, ROWS)] for _, row in tiles]
            ups = [up_in[step, pl.ds(row, ROWS)] for _, row in tiles]
            whens = [time_in[step, pl.ds(row, ROWS)] for _, row in tiles]
            if step < 3:
                lowers = uppers = values
            else:
                places = places_of(step, 0, rows_each, 0, 2 << step)
                lowers = [work[step - 3, at, pl.ds(row, ROWS)] for at in beams for _, _, row, _ in places]
                uppers = [work[step - 3, at, pl.ds(row, ROWS)] for at in beams for _, _, _, row in places]
            values = merge(lowers, uppers, lows, ups, whens, samples)
            if step >= 2:
                for (at, row), value in zip(tiles, values):
                    if step < local - 1:
                        work[step - 2, at, pl.ds(row, ROWS)] = value
                    else:
                        ready[at, pl.ds(row, ROWS)] = value

    per = max(1, BATCH * ROWS // rows_each)
    for at, (_, devices) in enumerate(order):
        for load in loads[at]:
            load.wait()
        beams = [device[0] * chan_count + device[1] for device in devices]
        for place in range(0, len(beams), per):
            dedisperse(beams[place : place + per])
        if at == 0:
            pl.semaphore_wait(barrier, count - 1)
        for piece in reversed(range(pieces)):
            rows = pl.ds(piece * piece_rows, piece_rows)
            for place, device in enumerate(devices):
                if (at, place) != (own, 0):
                    pltpu.make_async_remote_copy(
                        src_ref=ready.at[beams[place], rows],
                        dst_ref=got.at[me, rows],
                        send_sem=send_sem,
                        recv_sem=recv_sem.at[piece],
                        device_id=device,
                        device_id_type=MESH,
                    ).start()
    got[me] = ready[me]
    build_indices(range(local, levels), lower_ref[...], upper_ref[...], shift_ref[...], low_at, up_at, time_at, samples)

    for piece in reversed(range(pieces)):
        arrived = got.at[pl.ds(0, count - 1), pl.ds(0, piece_rows)]
        pltpu.make_async_copy(arrived, arrived, recv_sem.at[piece]).wait()
        for step in range(local, levels):
            part = (2 << step) // pieces
            places = places_of(step, 0, bands, piece * part, (piece + 1) * part)
            out = states[step - local]

            def read(row):
                if step == local:
                    return got[row // rows_each, pl.ds(row % rows_each, ROWS)]
                return states[step - local - 1][pl.ds(row, ROWS)]

            for at in range(0, len(places), BATCH):
                batch = places[at : at + BATCH]
                rows = [pl.ds(row, ROWS) for row, _, _, _ in batch]
                values = merge(
                    [read(row) for _, _, row, _ in batch],
                    [read(row) for _, _, _, row in batch],
                    [low_at[step - local, row] for row in rows],
                    [up_at[step - local, row] for row in rows],
                    [time_at[step - local, row] for row in rows],
                    samples,
                )
                for row, value in zip(rows, values):
                    out[row] = value
        size = bands // pieces
        scores(states[-1], piece * size, size, widths_ref, limit_ref, out_ref, samples)
    sent = ready.at[pl.ds(0, count - 1)]
    pltpu.make_async_copy(sent, sent, send_sem).wait()


def shards(intensities, lower_index, upper_index, delay_shift, widths, max_delay):
    beam_count = lax.axis_size("beam")
    chan_count = lax.axis_size("chan")
    count = beam_count * chan_count
    beams, channels, samples = intensities.shape
    rows_each = channels // SUB0
    bands = count * rows_each
    levels = lower_index.shape[0]
    local = rows_each.bit_length() - 1
    pieces = rows_each // ROWS
    return pl.pallas_call(
        functools.partial(kernel, beam_count, chan_count, levels, pieces),
        out_shape=pltpu.VMEM((1, widths.shape[0], bands), jnp.float32),
        in_specs=[pl.BlockSpec(memory_space=pltpu.HBM)] * 6,
        out_specs=pl.BlockSpec(memory_space=pltpu.VMEM),
        scratch_shapes=[
            pltpu.VMEM((beams, channels, samples), intensities.dtype),
            pltpu.VMEM(lower_index.shape, jnp.int32),
            pltpu.VMEM(upper_index.shape, jnp.int32),
            pltpu.VMEM(delay_shift.shape, jnp.int32),
            pltpu.SMEM(widths.shape, jnp.int32),
            pltpu.SMEM(max_delay.shape, jnp.int32),
            pltpu.VMEM((max(1, local - 3), count, rows_each, samples), jnp.float32),
            pltpu.VMEM((count, rows_each, samples), jnp.float32),
            pltpu.VMEM((count, rows_each, samples), jnp.float32),
        ]
        + [pltpu.VMEM((bands, samples), jnp.float32)] * (levels - local)
        + [pltpu.VMEM((local, rows_each, samples), jnp.int32)] * 3
        + [pltpu.VMEM((levels - local, bands, samples), jnp.int32)] * 3
        + [
            pltpu.SemaphoreType.DMA((chan_count // 2, beam_count)),
            pltpu.SemaphoreType.DMA((5,)),
            pltpu.SemaphoreType.DMA,
            pltpu.SemaphoreType.DMA((pieces,)),
        ],
        compiler_params=pltpu.CompilerParams(
            collective_id=0, has_side_effects=True, vmem_limit_bytes=56 * 1024 * 1024
        ),
        name="search",
    )(intensities, lower_index, upper_index, delay_shift, widths, max_delay)


def solution(mesh):
    in_specs = (P(None, ("beam", "chan"), None), P(), P(), P(), P(), P(("beam", "chan")))
    out_specs = P(("beam", "chan"), None, None)
    return jax.shard_map(shards, mesh=mesh, in_specs=in_specs, out_specs=out_specs, check_vma=False)
```

```python
import functools

import jax
import jax.numpy as jnp
from jax import lax
from jax.experimental import pallas as pl
from jax.experimental.pallas import tpu as pltpu
from jax.sharding import PartitionSpec as P

SUB0 = 8
ROWS = 8
BATCH = 16
MESH = pl.DeviceIdType.MESH


def take(values, index, axis):
    return jnp.take_along_axis(values, index, axis=axis, mode="promise_in_bounds")


def source_base(trial, width):
    half = width // 2
    return jnp.minimum(4 * (trial // ROWS), jnp.maximum(half - ROWS, 0))


def build_indices(steps, lower, upper, shift, low_at, up_at, time_at, samples):
    levels, bands = lower.shape
    kept = low_at.shape[1]
    depth = 16
    zeros = jnp.zeros((depth - levels, bands), jnp.int32)
    lower = jnp.concatenate([lower, zeros], axis=0)
    upper = jnp.concatenate([upper, zeros], axis=0)
    shift = jnp.concatenate([shift, zeros], axis=0)
    level = lax.broadcasted_iota(jnp.int32, (depth, bands), 0)
    row = lax.broadcasted_iota(jnp.int32, (depth, bands), 1)
    width = jnp.left_shift(jnp.int32(2), level)
    trial = row & (width - 1)
    inside = (row & (ROWS - 1)) - trial
    skip = source_base(trial, width)
    lower = jnp.where(level <= 2, inside + lower, lower - skip) & (ROWS - 1)
    upper = jnp.where(level <= 2, inside + width // 2 + upper, upper - skip) & (ROWS - 1)
    packed = jnp.concatenate(
        [(lower + ROWS * upper).astype(jnp.float32), jnp.minimum(shift, samples).astype(jnp.float32)],
        axis=0,
    ).astype(jnp.bfloat16)
    entry = lax.broadcasted_iota(jnp.int32, (2 * depth, samples), 0)
    time = lax.broadcasted_iota(jnp.int32, (kept, samples), 1)
    for at, step in enumerate(steps):
        spread = jnp.where(entry == step, 256.0, jnp.where(entry == depth + step, 1.0, 0.0))
        value = lax.dot_general(
            packed,
            spread.astype(jnp.bfloat16),
            (((0,), (0,)), ((), ())),
            preferred_element_type=jnp.float32,
        )[:kept].astype(jnp.int32)
        low_at[at] = (value >> 8) & (ROWS - 1)
        up_at[at] = value >> 11
        time_at[at] = time - (value & 255)


def merge(lowers, uppers, lows, ups, whens, samples):
    uppers = [take(v, up, 0) for v, up in zip(uppers, ups)]
    lowers = [take(v, low, 0) for v, low in zip(lowers, lows)]
    uppers = [take(v, when & (samples - 1), 1) for v, when in zip(uppers, whens)]
    return [v + jnp.where(when >= 0, u, 0.0) for v, u, when in zip(lowers, uppers, whens)]


def places_of(step, start, size, first, last):
    width = 2 << step
    places = []
    for base in range(0, size, width):
        for trial in range(first, last, ROWS):
            skip = min(4 * (trial // ROWS), max(width // 2 - ROWS, 0))
            places.append((base + trial, start + base + trial, start + base + skip, start + base + width // 2 + skip))
    return places


def build_boxes(widths_ref, boxes_ref):
    boxes, samples, _ = boxes_ref.shape
    source = lax.broadcasted_iota(jnp.int32, (samples, samples), 1)
    target = lax.broadcasted_iota(jnp.int32, (samples, samples), 0)
    back = target - source
    for box in range(boxes):
        width = widths_ref[box]
        hit = jnp.where((back >= 0) & (back < width), 1.0, 0.0)
        mean = jnp.minimum(width, samples - source).astype(jnp.float32) * (1.0 / samples)
        value = (hit - mean).astype(jnp.bfloat16)
        boxes_ref[box, :, pl.ds(0, samples)] = value
        boxes_ref[box, :, pl.ds(samples, samples)] = value


def scores(trials_ref, start, size, boxes_ref, limit_ref, out_ref):
    boxes, samples, _ = boxes_ref.shape
    chunk = min(256, size)
    limit = limit_ref[0]
    for at in range(start, start + size, chunk):
        trials = trials_ref[pl.ds(at, chunk)]
        high = trials.astype(jnp.bfloat16)
        low = (trials - high.astype(jnp.float32)).astype(jnp.bfloat16)
        both = jnp.concatenate([high, low], axis=1)
        tops, spreads = [], []
        for box in range(boxes):
            offset = lax.dot_general(
                boxes_ref[box], both, (((1,), (1,)), ((), ())), preferred_element_type=jnp.float32
            )
            tops.append(jnp.max(offset, axis=0, keepdims=True))
            spreads.append(jnp.sum(offset * offset, axis=0, keepdims=True))
        top = jnp.concatenate(tops, axis=0)
        spread = jnp.concatenate(spreads, axis=0) * (1.0 / samples)
        keep = lax.broadcasted_iota(jnp.int32, (boxes, chunk), 1) + at <= limit
        out_ref[0, :, pl.ds(at, chunk)] = jnp.where(keep, top / jnp.sqrt(spread + 1e-05), 0.0)


def schedule(groups, near, turns):
    cut = max(1, len(turns) // 2)
    later = [at for at in range(1, groups) if at not in near]
    items = [(0,)] + [(0, piece, 0) for piece in turns] + [(0, piece, 1) for piece in turns[:cut]]
    for at in later:
        items += [(at,)] + [(at, piece, 0) for piece in turns] + [(at, turns[0], 1)]
    for at in near:
        items += [(at,)] + [(at, piece, 2) for piece in turns[:cut]]
    for turn in range(1, len(turns)):
        ahead = turns[turn + cut - 1 : turn + cut]
        items += [(0, piece, 1) for piece in ahead]
        items += [(at, turns[turn], 1) for at in later]
        items += [(at, piece, 2) for at in near for piece in ahead]
    return items


def kernel(
    beam_count, chan_count, levels, pieces,
    x_hbm, lower_hbm, upper_hbm, shift_hbm, widths_hbm, limit_hbm, out_ref,
    x_ref, lower_ref, upper_ref, shift_ref, widths_ref, limit_ref, boxes_ref, work, ready, got, *rest,
):
    count = beam_count * chan_count
    channels, samples = x_ref.shape[1], x_ref.shape[2]
    rows_each = channels // SUB0
    bands = count * rows_each
    local = rows_each.bit_length() - 1
    states, rest = rest[: levels - local], rest[levels - local :]
    low_in, up_in, time_in, low_at, up_at, time_at, load_sem, table_sem, send_sem, recv_sem = rest
    beam, chan = lax.axis_index("beam"), lax.axis_index("chan")
    me = beam * chan_count + chan
    piece_rows = rows_each // pieces

    pair, core = chan // 2, chan % 2
    half = chan_count // 4
    side = pair // half
    far = [(1 - side) * half + at for at in range(half)]
    near = [side * half + (pair + 1 + at) % half for at in range(half)]
    beam_steps = [(1 << bit) * (1 - 2 * (beam // (1 << bit) % 2)) for bit in range(beam_count.bit_length() - 1)]

    def other_beam(mask):
        value = beam
        for bit, step in enumerate(beam_steps):
            if mask >> bit & 1:
                value = value + step
        return value

    def group(pair_to, beams):
        return [(at, pair_to * 2 + (core + turn) % 2) for at in beams for turn in range(2)]

    fixed = [jnp.int32(at) for at in range(beam_count)]
    turned = [other_beam(mask) for mask in range(beam_count)]
    order = [(far[0], group(far[0], fixed))]
    order += [(pair_to, group(pair_to, turned)) for pair_to in near]
    order += [(pair_to, group(pair_to, fixed)) for pair_to in far[1:]]
    own = half

    barrier = pltpu.get_barrier_semaphore()
    for at, (_, devices) in enumerate(order):
        for place, device in enumerate(devices):
            if (at, place) != (own, 0):
                pl.semaphore_signal(barrier, inc=1, device_id=device, device_id_type=MESH)
    others = [(lower_hbm, lower_ref), (upper_hbm, upper_ref), (shift_hbm, shift_ref), (widths_hbm, widths_ref), (limit_hbm, limit_ref)]
    tables = [pltpu.make_async_copy(source, target, table_sem.at[at]) for at, (source, target) in enumerate(others)]
    for table in tables:
        table.start()
    loads = []
    for at, (pair_to, _) in enumerate(order):
        loads.append([])
        for mask in range(beam_count):
            rows = pl.ds(other_beam(mask) * chan_count + pair_to * 2, 2)
            load = pltpu.make_async_copy(x_hbm.at[rows], x_ref.at[rows], load_sem.at[at, mask])
            load.start()
            loads[-1].append(load)
    band = lax.broadcasted_iota(jnp.int32, (rows_each, channels), 0)
    channel = lax.broadcasted_iota(jnp.int32, (rows_each, channels), 1)
    adder = jnp.where(channel // SUB0 == band, 1.0, 0.0).astype(jnp.bfloat16)
    for table in tables:
        table.wait()
    block = 128
    first = me * rows_each
    lanes = pl.ds(pl.multiple_of(first // block * block, block), block)
    away = (block - first % block) % block
    mine = [pltpu.roll(ref[:, lanes], away, 1) for ref in (lower_ref, upper_ref, shift_ref)]
    build_indices(range(local), *mine, low_in, up_in, time_in, samples)

    def dedisperse(beams):
        sums = [jnp.dot(adder, x_ref[at], preferred_element_type=jnp.float32) for at in beams]
        tiles = [(at, row) for at in beams for row in range(0, rows_each, ROWS)]
        values = [v[row : row + ROWS] for v in sums for row in range(0, rows_each, ROWS)]
        for step in range(local):
            lows = [low_in[step, pl.ds(row, ROWS)] for _, row in tiles]
            ups = [up_in[step, pl.ds(row, ROWS)] for _, row in tiles]
            whens = [time_in[step, pl.ds(row, ROWS)] for _, row in tiles]
            if step < 3:
                lowers = uppers = values
            else:
                places = places_of(step, 0, rows_each, 0, 2 << step)
                lowers = [work[step - 3, at, pl.ds(row, ROWS)] for at in beams for _, _, row, _ in places]
                uppers = [work[step - 3, at, pl.ds(row, ROWS)] for at in beams for _, _, _, row in places]
            values = merge(lowers, uppers, lows, ups, whens, samples)
            if step >= 2:
                for (at, row), value in zip(tiles, values):
                    if step < local - 1:
                        work[step - 2, at, pl.ds(row, ROWS)] = value
                    else:
                        ready[at, pl.ds(row, ROWS)] = value

    def send(at, place, piece):
        device = order[at][1][place]
        rows = pl.ds(piece * piece_rows, piece_rows)
        pltpu.make_async_remote_copy(
            src_ref=ready.at[device[0] * chan_count + device[1], rows],
            dst_ref=got.at[me, rows],
            send_sem=send_sem,
            recv_sem=recv_sem.at[piece],
            device_id=device,
            device_id_type=MESH,
        ).start()

    def compute(at):
        for load in loads[at]:
            load.wait()
        beams = [device[0] * chan_count + device[1] for device in order[at][1]]
        for place in range(0, len(beams), per):
            dedisperse(beams[place : place + per])

    per = max(1, BATCH * ROWS // rows_each)
    turns = list(reversed(range(pieces)))
    greeted = False
    for item in schedule(len(order), range(1, half + 1), turns):
        if len(item) == 1:
            compute(item[0])
            continue
        if not greeted:
            pl.semaphore_wait(barrier, count - 1)
            greeted = True
        at, piece, part = item
        for to in (range(2), range(2, 2 * beam_count), range(2 * beam_count))[part]:
            if (at, to) != (own, 0):
                send(at, to, piece)
    got[me] = ready[me]
    build_boxes(widths_ref, boxes_ref)
    build_indices(range(local, levels), lower_ref[...], upper_ref[...], shift_ref[...], low_at, up_at, time_at, samples)

    for piece in turns:
        arrived = got.at[pl.ds(0, count - 1), pl.ds(0, piece_rows)]
        pltpu.make_async_copy(arrived, arrived, recv_sem.at[piece]).wait()
        for step in range(local, levels):
            part = (2 << step) // pieces
            places = places_of(step, 0, bands, piece * part, (piece + 1) * part)
            out = states[step - local]

            def read(row):
                if step == local:
                    return got[row // rows_each, pl.ds(row % rows_each, ROWS)]
                return states[step - local - 1][pl.ds(row, ROWS)]

            for at in range(0, len(places), BATCH):
                batch = places[at : at + BATCH]
                rows = [pl.ds(row, ROWS) for row, _, _, _ in batch]
                values = merge(
                    [read(row) for _, _, row, _ in batch],
                    [read(row) for _, _, _, row in batch],
                    [low_at[step - local, row] for row in rows],
                    [up_at[step - local, row] for row in rows],
                    [time_at[step - local, row] for row in rows],
                    samples,
                )
                for row, value in zip(rows, values):
                    out[row] = value
        size = bands // pieces
        scores(states[-1], piece * size, size, boxes_ref, limit_ref, out_ref)
    sent = ready.at[pl.ds(0, count - 1)]
    pltpu.make_async_copy(sent, sent, send_sem).wait()


def shards(intensities, lower_index, upper_index, delay_shift, widths, max_delay):
    beam_count = lax.axis_size("beam")
    chan_count = lax.axis_size("chan")
    count = beam_count * chan_count
    beams, channels, samples = intensities.shape
    rows_each = channels // SUB0
    bands = count * rows_each
    levels = lower_index.shape[0]
    local = rows_each.bit_length() - 1
    pieces = rows_each // ROWS
    return pl.pallas_call(
        functools.partial(kernel, beam_count, chan_count, levels, pieces),
        out_shape=pltpu.VMEM((1, widths.shape[0], bands), jnp.float32),
        in_specs=[pl.BlockSpec(memory_space=pltpu.HBM)] * 6,
        out_specs=pl.BlockSpec(memory_space=pltpu.VMEM),
        scratch_shapes=[
            pltpu.VMEM((beams, channels, samples), intensities.dtype),
            pltpu.VMEM(lower_index.shape, jnp.int32),
            pltpu.VMEM(upper_index.shape, jnp.int32),
            pltpu.VMEM(delay_shift.shape, jnp.int32),
            pltpu.SMEM(widths.shape, jnp.int32),
            pltpu.SMEM(max_delay.shape, jnp.int32),
            pltpu.VMEM((widths.shape[0], samples, 2 * samples), jnp.bfloat16),
            pltpu.VMEM((max(1, local - 3), count, rows_each, samples), jnp.float32),
            pltpu.VMEM((count, rows_each, samples), jnp.float32),
            pltpu.VMEM((count, rows_each, samples), jnp.float32),
        ]
        + [pltpu.VMEM((bands, samples), jnp.float32)] * (levels - local)
        + [pltpu.VMEM((local, rows_each, samples), jnp.int32)] * 3
        + [pltpu.VMEM((levels - local, bands, samples), jnp.int32)] * 3
        + [
            pltpu.SemaphoreType.DMA((chan_count // 2, beam_count)),
            pltpu.SemaphoreType.DMA((5,)),
            pltpu.SemaphoreType.DMA,
            pltpu.SemaphoreType.DMA((pieces,)),
        ],
        compiler_params=pltpu.CompilerParams(
            collective_id=0, has_side_effects=True, vmem_limit_bytes=56 * 1024 * 1024
        ),
        name="search",
    )(intensities, lower_index, upper_index, delay_shift, widths, max_delay)


def solution(mesh):
    in_specs = (P(None, ("beam", "chan"), None), P(), P(), P(), P(), P(("beam", "chan")))
    out_specs = P(("beam", "chan"), None, None)
    return jax.shard_map(shards, mesh=mesh, in_specs=in_specs, out_specs=out_specs, check_vma=False)
```

```python
import functools

import jax
import jax.numpy as jnp
from jax import lax
from jax.experimental import pallas as pl
from jax.experimental.pallas import tpu as pltpu
from jax.sharding import PartitionSpec as P

SUB0 = 8
ROWS = 8
BATCH = 16
MESH = pl.DeviceIdType.MESH


def take(values, index, axis):
    return jnp.take_along_axis(values, index, axis=axis, mode="promise_in_bounds")


def source_base(trial, width):
    half = width // 2
    return jnp.minimum(4 * (trial // ROWS), jnp.maximum(half - ROWS, 0))


def build_indices(steps, lower, upper, shift, low_at, up_at, time_at, samples):
    levels, bands = lower.shape
    kept = low_at.shape[1]
    depth = 16
    zeros = jnp.zeros((depth - levels, bands), jnp.int32)
    lower = jnp.concatenate([lower, zeros], axis=0)
    upper = jnp.concatenate([upper, zeros], axis=0)
    shift = jnp.concatenate([shift, zeros], axis=0)
    level = lax.broadcasted_iota(jnp.int32, (depth, bands), 0)
    row = lax.broadcasted_iota(jnp.int32, (depth, bands), 1)
    width = jnp.left_shift(jnp.int32(2), level)
    trial = row & (width - 1)
    inside = (row & (ROWS - 1)) - trial
    skip = source_base(trial, width)
    lower = jnp.where(level <= 2, inside + lower, lower - skip) & (ROWS - 1)
    upper = jnp.where(level <= 2, inside + width // 2 + upper, upper - skip) & (ROWS - 1)
    packed = jnp.concatenate(
        [(lower + ROWS * upper).astype(jnp.float32), jnp.minimum(shift, samples).astype(jnp.float32)],
        axis=0,
    ).astype(jnp.bfloat16)
    entry = lax.broadcasted_iota(jnp.int32, (2 * depth, samples), 0)
    time = lax.broadcasted_iota(jnp.int32, (kept, samples), 1)
    for at, step in enumerate(steps):
        spread = jnp.where(entry == step, 256.0, jnp.where(entry == depth + step, 1.0, 0.0))
        value = lax.dot_general(
            packed,
            spread.astype(jnp.bfloat16),
            (((0,), (0,)), ((), ())),
            preferred_element_type=jnp.float32,
        )[:kept].astype(jnp.int32)
        low_at[at] = (value >> 8) & (ROWS - 1)
        up_at[at] = value >> 11
        time_at[at] = time - (value & 255)


def merge(lowers, uppers, lows, ups, whens, samples):
    uppers = [take(v, up, 0) for v, up in zip(uppers, ups)]
    lowers = [take(v, low, 0) for v, low in zip(lowers, lows)]
    uppers = [take(v, when & (samples - 1), 1) for v, when in zip(uppers, whens)]
    return [v + jnp.where(when >= 0, u, 0.0) for v, u, when in zip(lowers, uppers, whens)]


def places_of(step, start, size, first, last):
    width = 2 << step
    places = []
    for base in range(0, size, width):
        for trial in range(first, last, ROWS):
            skip = min(4 * (trial // ROWS), max(width // 2 - ROWS, 0))
            places.append((base + trial, start + base + trial, start + base + skip, start + base + width // 2 + skip))
    return places


def build_boxes(widths_ref, boxes_ref):
    boxes, samples, _ = boxes_ref.shape
    source = lax.broadcasted_iota(jnp.int32, (samples, samples), 1)
    target = lax.broadcasted_iota(jnp.int32, (samples, samples), 0)
    back = target - source
    for box in range(boxes):
        width = widths_ref[box]
        hit = jnp.where((back >= 0) & (back < width), 1.0, 0.0)
        mean = jnp.minimum(width, samples - source).astype(jnp.float32) * (1.0 / samples)
        value = (hit - mean).astype(jnp.bfloat16)
        boxes_ref[box, :, pl.ds(0, samples)] = value
        boxes_ref[box, :, pl.ds(samples, samples)] = value


def scores(trials_ref, start, size, boxes_ref, limit_ref, out_ref):
    boxes, samples, _ = boxes_ref.shape
    chunk = min(256, size)
    limit = limit_ref[0]
    for at in range(start, start + size, chunk):
        trials = trials_ref[pl.ds(at, chunk)]
        high = trials.astype(jnp.bfloat16)
        low = (trials - high.astype(jnp.float32)).astype(jnp.bfloat16)
        both = jnp.concatenate([high, low], axis=1)
        tops, spreads = [], []
        for box in range(boxes):
            offset = lax.dot_general(
                boxes_ref[box], both, (((1,), (1,)), ((), ())), preferred_element_type=jnp.float32
            )
            tops.append(jnp.max(offset, axis=0, keepdims=True))
            spreads.append(jnp.sum(offset * offset, axis=0, keepdims=True))
        top = jnp.concatenate(tops, axis=0)
        spread = jnp.concatenate(spreads, axis=0) * (1.0 / samples)
        keep = lax.broadcasted_iota(jnp.int32, (boxes, chunk), 1) + at <= limit
        out_ref[0, :, pl.ds(at, chunk)] = jnp.where(keep, top / jnp.sqrt(spread + 1e-05), 0.0)


def schedule(groups, near, turns):
    cut = max(1, len(turns) // 2)
    later = [at for at in range(1, groups) if at not in near]
    items = [(0, 0)] + [(0, piece, 0) for piece in turns] + [(0, 1)] + [(0, piece, 1) for piece in turns[:cut]]
    for at in later:
        items += [(at, 2), (at, turns[0], 0), (at, turns[0], 1)] + [(at, piece, 0) for piece in turns[1:2]]
    for at in near:
        items += [(at, 2)] + [(at, piece, 2) for piece in turns[:cut]]
    for turn in range(1, len(turns)):
        ahead = turns[turn + cut - 1 : turn + cut]
        items += [(0, piece, 1) for piece in ahead]
        for at in later:
            items += [(at, turns[turn], 1)] + [(at, piece, 0) for piece in turns[turn + 1 : turn + 2]]
        items += [(at, piece, 2) for at in near for piece in ahead]
    return items


def kernel(
    beam_count, chan_count, levels, pieces,
    x_hbm, lower_hbm, upper_hbm, shift_hbm, widths_hbm, limit_hbm, out_ref,
    x_ref, lower_ref, upper_ref, shift_ref, widths_ref, limit_ref, boxes_ref, work, ready, got, *rest,
):
    count = beam_count * chan_count
    channels, samples = x_ref.shape[1], x_ref.shape[2]
    rows_each = channels // SUB0
    bands = count * rows_each
    local = rows_each.bit_length() - 1
    states, rest = rest[: levels - local], rest[levels - local :]
    low_in, up_in, time_in, low_at, up_at, time_at, load_sem, table_sem, send_sem, recv_sem = rest
    beam, chan = lax.axis_index("beam"), lax.axis_index("chan")
    me = beam * chan_count + chan
    piece_rows = rows_each // pieces

    pair, core = chan // 2, chan % 2
    half = chan_count // 4
    side = pair // half
    far = [(1 - side) * half + at for at in range(half)]
    near = [side * half + (pair + 1 + at) % half for at in range(half)]
    beam_steps = [(1 << bit) * (1 - 2 * (beam // (1 << bit) % 2)) for bit in range(beam_count.bit_length() - 1)]

    def other_beam(mask):
        value = beam
        for bit, step in enumerate(beam_steps):
            if mask >> bit & 1:
                value = value + step
        return value

    def group(pair_to, beams):
        return [(at, pair_to * 2 + (core + turn) % 2) for at in beams for turn in range(2)]

    fixed = [jnp.int32(at) for at in range(beam_count)]
    turned = [other_beam(mask) for mask in range(beam_count)]
    order = [(far[0], group(far[0], fixed))]
    order += [(pair_to, group(pair_to, turned)) for pair_to in near]
    order += [(pair_to, group(pair_to, fixed)) for pair_to in far[1:]]
    own = half

    barrier = pltpu.get_barrier_semaphore()
    loads = []
    for at, (pair_to, devices) in enumerate(order):
        loads.append([])
        for place in range(0, len(devices), 2):
            rows = pl.ds(devices[place][0] * chan_count + pair_to * 2, 2)
            loads[-1].append(pltpu.make_async_copy(x_hbm.at[rows], x_ref.at[rows], load_sem.at[at, place // 2]))
    others = [(lower_hbm, lower_ref), (upper_hbm, upper_ref), (shift_hbm, shift_ref), (widths_hbm, widths_ref), (limit_hbm, limit_ref)]
    tables = [pltpu.make_async_copy(source, target, table_sem.at[at]) for at, (source, target) in enumerate(others)]
    for table in tables:
        table.start()
    for load in loads[0]:
        load.start()
    for at, (_, devices) in enumerate(order):
        for place, device in enumerate(devices):
            if (at, place) != (own, 0):
                pl.semaphore_signal(barrier, inc=1, device_id=device, device_id_type=MESH)
    for group_loads in loads[1:]:
        for load in group_loads:
            load.start()

    band = lax.broadcasted_iota(jnp.int32, (rows_each, channels), 0)
    channel = lax.broadcasted_iota(jnp.int32, (rows_each, channels), 1)
    adder = jnp.where(channel // SUB0 == band, 1.0, 0.0).astype(jnp.bfloat16)
    for table in tables:
        table.wait()
    block = 128
    first = me * rows_each
    lanes = pl.ds(pl.multiple_of(first // block * block, block), block)
    away = (block - first % block) % block
    mine = [pltpu.roll(ref[:, lanes], away, 1) for ref in (lower_ref, upper_ref, shift_ref)]
    build_indices(range(local), *mine, low_in, up_in, time_in, samples)

    def dedisperse(beams):
        sums = [jnp.dot(adder, x_ref[at], preferred_element_type=jnp.float32) for at in beams]
        tiles = [(at, row) for at in beams for row in range(0, rows_each, ROWS)]
        values = [v[row : row + ROWS] for v in sums for row in range(0, rows_each, ROWS)]
        for step in range(local):
            lows = [low_in[step, pl.ds(row, ROWS)] for _, row in tiles]
            ups = [up_in[step, pl.ds(row, ROWS)] for _, row in tiles]
            whens = [time_in[step, pl.ds(row, ROWS)] for _, row in tiles]
            if step < 3:
                lowers = uppers = values
            else:
                places = places_of(step, 0, rows_each, 0, 2 << step)
                lowers = [work[step - 3, at, pl.ds(row, ROWS)] for at in beams for _, _, row, _ in places]
                uppers = [work[step - 3, at, pl.ds(row, ROWS)] for at in beams for _, _, _, row in places]
            values = merge(lowers, uppers, lows, ups, whens, samples)
            if step >= 2:
                for (at, row), value in zip(tiles, values):
                    if step < local - 1:
                        work[step - 2, at, pl.ds(row, ROWS)] = value
                    else:
                        ready[at, pl.ds(row, ROWS)] = value

    def send(at, place, piece):
        device = order[at][1][place]
        rows = pl.ds(piece * piece_rows, piece_rows)
        pltpu.make_async_remote_copy(
            src_ref=ready.at[device[0] * chan_count + device[1], rows],
            dst_ref=got.at[me, rows],
            send_sem=send_sem,
            recv_sem=recv_sem.at[piece],
            device_id=device,
            device_id_type=MESH,
        ).start()

    def compute(at, part):
        for mask in sorted({place // 2 for place in parts[part]}):
            loads[at][mask].wait()
        beams = [device[0] * chan_count + device[1] for device in order[at][1]]
        for first in range(parts[part].start, parts[part].stop, per):
            dedisperse(beams[first : min(first + per, parts[part].stop)])

    parts = (range(2), range(2, 2 * beam_count), range(2 * beam_count))
    per = max(1, BATCH * ROWS // rows_each)
    turns = list(reversed(range(pieces)))
    greeted = False
    for item in schedule(len(order), range(1, half + 1), turns):
        if len(item) == 2:
            compute(*item)
            continue
        if not greeted:
            pl.semaphore_wait(barrier, count - 1)
            greeted = True
        at, piece, part = item
        for to in parts[part]:
            if (at, to) != (own, 0):
                send(at, to, piece)
    got[me] = ready[me]
    build_boxes(widths_ref, boxes_ref)
    build_indices(range(local, levels), lower_ref[...], upper_ref[...], shift_ref[...], low_at, up_at, time_at, samples)

    for piece in turns:
        arrived = got.at[pl.ds(0, count - 1), pl.ds(0, piece_rows)]
        pltpu.make_async_copy(arrived, arrived, recv_sem.at[piece]).wait()
        for step in range(local, levels):
            part = (2 << step) // pieces
            places = places_of(step, 0, bands, piece * part, (piece + 1) * part)
            out = states[step - local]

            def read(row):
                if step == local:
                    return got[row // rows_each, pl.ds(row % rows_each, ROWS)]
                return states[step - local - 1][pl.ds(row, ROWS)]

            for at in range(0, len(places), BATCH):
                batch = places[at : at + BATCH]
                rows = [pl.ds(row, ROWS) for row, _, _, _ in batch]
                values = merge(
                    [read(row) for _, _, row, _ in batch],
                    [read(row) for _, _, _, row in batch],
                    [low_at[step - local, row] for row in rows],
                    [up_at[step - local, row] for row in rows],
                    [time_at[step - local, row] for row in rows],
                    samples,
                )
                for row, value in zip(rows, values):
                    out[row] = value
        size = bands // pieces
        scores(states[-1], piece * size, size, boxes_ref, limit_ref, out_ref)
    sent = ready.at[pl.ds(0, count - 1)]
    pltpu.make_async_copy(sent, sent, send_sem).wait()


def shards(intensities, lower_index, upper_index, delay_shift, widths, max_delay):
    beam_count = lax.axis_size("beam")
    chan_count = lax.axis_size("chan")
    count = beam_count * chan_count
    beams, channels, samples = intensities.shape
    rows_each = channels // SUB0
    bands = count * rows_each
    levels = lower_index.shape[0]
    local = rows_each.bit_length() - 1
    pieces = rows_each // ROWS
    return pl.pallas_call(
        functools.partial(kernel, beam_count, chan_count, levels, pieces),
        out_shape=pltpu.VMEM((1, widths.shape[0], bands), jnp.float32),
        in_specs=[pl.BlockSpec(memory_space=pltpu.HBM)] * 6,
        out_specs=pl.BlockSpec(memory_space=pltpu.VMEM),
        scratch_shapes=[
            pltpu.VMEM((beams, channels, samples), intensities.dtype),
            pltpu.VMEM(lower_index.shape, jnp.int32),
            pltpu.VMEM(upper_index.shape, jnp.int32),
            pltpu.VMEM(delay_shift.shape, jnp.int32),
            pltpu.SMEM(widths.shape, jnp.int32),
            pltpu.SMEM(max_delay.shape, jnp.int32),
            pltpu.VMEM((widths.shape[0], samples, 2 * samples), jnp.bfloat16),
            pltpu.VMEM((max(1, local - 3), count, rows_each, samples), jnp.float32),
            pltpu.VMEM((count, rows_each, samples), jnp.float32),
            pltpu.VMEM((count, rows_each, samples), jnp.float32),
        ]
        + [pltpu.VMEM((bands, samples), jnp.float32)] * (levels - local)
        + [pltpu.VMEM((local, rows_each, samples), jnp.int32)] * 3
        + [pltpu.VMEM((levels - local, bands, samples), jnp.int32)] * 3
        + [
            pltpu.SemaphoreType.DMA((chan_count // 2, beam_count)),
            pltpu.SemaphoreType.DMA((5,)),
            pltpu.SemaphoreType.DMA,
            pltpu.SemaphoreType.DMA((pieces,)),
        ],
        compiler_params=pltpu.CompilerParams(
            collective_id=0, has_side_effects=True, vmem_limit_bytes=56 * 1024 * 1024
        ),
        name="search",
    )(intensities, lower_index, upper_index, delay_shift, widths, max_delay)


def solution(mesh):
    in_specs = (P(None, ("beam", "chan"), None), P(), P(), P(), P(), P(("beam", "chan")))
    out_specs = P(("beam", "chan"), None, None)
    return jax.shard_map(shards, mesh=mesh, in_specs=in_specs, out_specs=out_specs, check_vma=False)
```

```python
import functools

import jax
import jax.numpy as jnp
from jax import lax
from jax.experimental import pallas as pl
from jax.experimental.pallas import tpu as pltpu
from jax.sharding import PartitionSpec as P

SUB0 = 8
ROWS = 8
BATCH = 16
MESH = pl.DeviceIdType.MESH


def take(values, index, axis):
    return jnp.take_along_axis(values, index, axis=axis, mode="promise_in_bounds")


def source_base(trial, width):
    half = width // 2
    return jnp.minimum(4 * (trial // ROWS), jnp.maximum(half - ROWS, 0))


def build_indices(steps, lower, upper, shift, low_at, up_at, time_at, samples):
    levels, bands = lower.shape
    kept = low_at.shape[1]
    depth = 16
    zeros = jnp.zeros((depth - levels, bands), jnp.int32)
    lower = jnp.concatenate([lower, zeros], axis=0)
    upper = jnp.concatenate([upper, zeros], axis=0)
    shift = jnp.concatenate([shift, zeros], axis=0)
    level = lax.broadcasted_iota(jnp.int32, (depth, bands), 0)
    row = lax.broadcasted_iota(jnp.int32, (depth, bands), 1)
    width = jnp.left_shift(jnp.int32(2), level)
    trial = row & (width - 1)
    inside = (row & (ROWS - 1)) - trial
    skip = source_base(trial, width)
    lower = jnp.where(level <= 2, inside + lower, lower - skip) & (ROWS - 1)
    upper = jnp.where(level <= 2, inside + width // 2 + upper, upper - skip) & (ROWS - 1)
    packed = jnp.concatenate(
        [(lower + ROWS * upper).astype(jnp.float32), jnp.minimum(shift, samples).astype(jnp.float32)],
        axis=0,
    ).astype(jnp.bfloat16)
    entry = lax.broadcasted_iota(jnp.int32, (2 * depth, samples), 0)
    time = lax.broadcasted_iota(jnp.int32, (kept, samples), 1)
    for at, step in enumerate(steps):
        spread = jnp.where(entry == step, 256.0, jnp.where(entry == depth + step, 1.0, 0.0))
        value = lax.dot_general(
            packed,
            spread.astype(jnp.bfloat16),
            (((0,), (0,)), ((), ())),
            preferred_element_type=jnp.float32,
        )[:kept].astype(jnp.int32)
        low_at[at] = (value >> 8) & (ROWS - 1)
        up_at[at] = value >> 11
        time_at[at] = time - (value & 255)


def merge(lowers, uppers, lows, ups, whens, samples):
    uppers = [take(v, up, 0) for v, up in zip(uppers, ups)]
    lowers = [take(v, low, 0) for v, low in zip(lowers, lows)]
    uppers = [take(v, when & (samples - 1), 1) for v, when in zip(uppers, whens)]
    return [v + jnp.where(when >= 0, u, 0.0) for v, u, when in zip(lowers, uppers, whens)]


def places_of(step, start, size, first, last):
    width = 2 << step
    places = []
    for base in range(0, size, width):
        for trial in range(first, last, ROWS):
            skip = min(4 * (trial // ROWS), max(width // 2 - ROWS, 0))
            places.append((base + trial, start + base + trial, start + base + skip, start + base + width // 2 + skip))
    return places


def build_boxes(widths_ref, boxes_ref):
    boxes, samples, _ = boxes_ref.shape
    source = lax.broadcasted_iota(jnp.int32, (samples, samples), 1)
    target = lax.broadcasted_iota(jnp.int32, (samples, samples), 0)
    back = target - source
    for box in range(boxes):
        width = widths_ref[box]
        hit = jnp.where((back >= 0) & (back < width), 1.0, 0.0)
        mean = jnp.minimum(width, samples - source).astype(jnp.float32) * (1.0 / samples)
        value = (hit - mean).astype(jnp.bfloat16)
        boxes_ref[box, :, pl.ds(0, samples)] = value
        boxes_ref[box, :, pl.ds(samples, samples)] = value


def scores(trials_ref, start, size, boxes_ref, limit_ref, out_ref):
    boxes, samples, _ = boxes_ref.shape
    chunk = min(256, size)
    steps = []

    def add(at):
        both, tops, spreads = [], [], []

        def split():
            trials = trials_ref[pl.ds(at, chunk)]
            high = trials.astype(jnp.bfloat16)
            low = (trials - high.astype(jnp.float32)).astype(jnp.bfloat16)
            both.append(jnp.concatenate([high, low], axis=1))

        def one(box):
            offset = lax.dot_general(
                boxes_ref[box], both[0], (((1,), (1,)), ((), ())), preferred_element_type=jnp.float32
            )
            tops.append(jnp.max(offset, axis=0, keepdims=True))
            spreads.append(jnp.sum(offset * offset, axis=0, keepdims=True))

        def finish():
            top = jnp.concatenate(tops, axis=0)
            spread = jnp.concatenate(spreads, axis=0) * (1.0 / samples)
            keep = lax.broadcasted_iota(jnp.int32, (boxes, chunk), 1) + at <= limit_ref[0]
            out_ref[0, :, pl.ds(at, chunk)] = jnp.where(keep, top / jnp.sqrt(spread + 1e-05), 0.0)

        steps.extend([split] + [functools.partial(one, box) for box in range(boxes)] + [finish])

    for at in range(start, start + size, chunk):
        add(at)
    return steps


def schedule(groups, near, turns):
    cut = max(1, len(turns) // 2)
    later = [at for at in range(1, groups) if at not in near]
    items = [(0, 0)] + [(0, piece, 0) for piece in turns] + [(0, 1)] + [(0, piece, 1) for piece in turns[:cut]]
    for at in later:
        items += [(at, 2), (at, turns[0], 0), (at, turns[0], 1)] + [(at, piece, 0) for piece in turns[1:2]]
    for at in near:
        items += [(at, 2)] + [(at, piece, 2) for piece in turns[:cut]]
    for turn in range(1, len(turns)):
        ahead = turns[turn + cut - 1 : turn + cut]
        items += [(0, piece, 1) for piece in ahead]
        for at in later:
            items += [(at, turns[turn], 1)] + [(at, piece, 0) for piece in turns[turn + 1 : turn + 2]]
        items += [(at, piece, 2) for at in near for piece in ahead]
    return items


def kernel(
    beam_count, chan_count, levels, pieces,
    x_hbm, lower_hbm, upper_hbm, shift_hbm, widths_hbm, limit_hbm, out_ref,
    x_ref, lower_ref, upper_ref, shift_ref, widths_ref, limit_ref, boxes_ref, work, ready, got, *rest,
):
    count = beam_count * chan_count
    channels, samples = x_ref.shape[1], x_ref.shape[2]
    rows_each = channels // SUB0
    bands = count * rows_each
    local = rows_each.bit_length() - 1
    states, rest = rest[: levels - local], rest[levels - local :]
    low_in, up_in, time_in, low_at, up_at, time_at, load_sem, table_sem, send_sem, recv_sem = rest
    beam, chan = lax.axis_index("beam"), lax.axis_index("chan")
    me = beam * chan_count + chan
    piece_rows = rows_each // pieces

    pair, core = chan // 2, chan % 2
    half = chan_count // 4
    side = pair // half
    far = [(1 - side) * half + at for at in range(half)]
    near = [side * half + (pair + 1 + at) % half for at in range(half)]
    beam_steps = [(1 << bit) * (1 - 2 * (beam // (1 << bit) % 2)) for bit in range(beam_count.bit_length() - 1)]

    def other_beam(mask):
        value = beam
        for bit, step in enumerate(beam_steps):
            if mask >> bit & 1:
                value = value + step
        return value

    def group(pair_to, beams, lead):
        return [(at, pair_to * 2 + (lead + turn) % 2) for at in beams for turn in range(2)]

    fixed = [jnp.int32(at) for at in range(beam_count)]
    turned = [other_beam(mask) for mask in range(beam_count)]
    order = [(far[0], group(far[0], fixed, 1))]
    order += [(pair_to, group(pair_to, turned, core)) for pair_to in near]
    order += [(pair_to, group(pair_to, fixed, 1)) for pair_to in far[1:]]
    own = half

    barrier = pltpu.get_barrier_semaphore()
    loads = []
    for at, (pair_to, devices) in enumerate(order):
        loads.append([])
        for place in range(0, len(devices), 2):
            rows = pl.ds(devices[place][0] * chan_count + pair_to * 2, 2)
            loads[-1].append(pltpu.make_async_copy(x_hbm.at[rows], x_ref.at[rows], load_sem.at[at, place // 2]))
    others = [(lower_hbm, lower_ref), (upper_hbm, upper_ref), (shift_hbm, shift_ref), (widths_hbm, widths_ref), (limit_hbm, limit_ref)]
    tables = [pltpu.make_async_copy(source, target, table_sem.at[at]) for at, (source, target) in enumerate(others)]
    for table in tables:
        table.start()
    for load in loads[0]:
        load.start()
    for at, (_, devices) in enumerate(order):
        for place, device in enumerate(devices):
            if (at, place) != (own, 0):
                pl.semaphore_signal(barrier, inc=1, device_id=device, device_id_type=MESH)
    for group_loads in loads[1:]:
        for load in group_loads:
            load.start()

    band = lax.broadcasted_iota(jnp.int32, (rows_each, channels), 0)
    channel = lax.broadcasted_iota(jnp.int32, (rows_each, channels), 1)
    adder = jnp.where(channel // SUB0 == band, 1.0, 0.0).astype(jnp.bfloat16)
    for table in tables:
        table.wait()
    block = 128
    first = me * rows_each
    lanes = pl.ds(pl.multiple_of(first // block * block, block), block)
    away = (block - first % block) % block
    mine = [pltpu.roll(ref[:, lanes], away, 1) for ref in (lower_ref, upper_ref, shift_ref)]
    build_indices(range(local), *mine, low_in, up_in, time_in, samples)

    def dedisperse(beams):
        sums = []
        for at in range(0, len(beams), 2):
            both = jnp.concatenate([x_ref[beam_at] for beam_at in beams[at : at + 2]], axis=1)
            both = jnp.dot(adder, both, preferred_element_type=jnp.float32)
            sums += [both[:, lane : lane + samples] for lane in range(0, both.shape[1], samples)]
        tiles = [(at, row) for at in beams for row in range(0, rows_each, ROWS)]
        values = [v[row : row + ROWS] for v in sums for row in range(0, rows_each, ROWS)]
        for step in range(local):
            lows = [low_in[step, pl.ds(row, ROWS)] for _, row in tiles]
            ups = [up_in[step, pl.ds(row, ROWS)] for _, row in tiles]
            whens = [time_in[step, pl.ds(row, ROWS)] for _, row in tiles]
            if step < 3:
                lowers = uppers = values
            else:
                places = places_of(step, 0, rows_each, 0, 2 << step)
                lowers = [work[step - 3, at, pl.ds(row, ROWS)] for at in beams for _, _, row, _ in places]
                uppers = [work[step - 3, at, pl.ds(row, ROWS)] for at in beams for _, _, _, row in places]
            values = merge(lowers, uppers, lows, ups, whens, samples)
            if step >= 2:
                for (at, row), value in zip(tiles, values):
                    if step < local - 1:
                        work[step - 2, at, pl.ds(row, ROWS)] = value
                    else:
                        ready[at, pl.ds(row, ROWS)] = value

    def send(at, place, piece):
        device = order[at][1][place]
        rows = pl.ds(piece * piece_rows, piece_rows)
        pltpu.make_async_remote_copy(
            src_ref=ready.at[device[0] * chan_count + device[1], rows],
            dst_ref=got.at[me, rows],
            send_sem=send_sem,
            recv_sem=recv_sem.at[piece],
            device_id=device,
            device_id_type=MESH,
        ).start()

    def compute(at, part):
        for mask in sorted({place // 2 for place in parts[part]}):
            loads[at][mask].wait()
        beams = [device[0] * chan_count + device[1] for device in order[at][1]]
        for first in range(parts[part].start, parts[part].stop, per):
            dedisperse(beams[first : min(first + per, parts[part].stop)])

    parts = (range(2), range(2, 2 * beam_count), range(2 * beam_count))
    per = max(1, BATCH * ROWS // rows_each)
    turns = list(reversed(range(pieces)))
    greeted = False
    for item in schedule(len(order), range(1, half + 1), turns):
        if len(item) == 2:
            compute(*item)
            continue
        if not greeted:
            pl.semaphore_wait(barrier, count - 1)
            greeted = True
        at, piece, part = item
        for to in parts[part]:
            if (at, to) != (own, 0):
                send(at, to, piece)
    got[me] = ready[me]
    build_boxes(widths_ref, boxes_ref)
    build_indices(range(local, levels), lower_ref[...], upper_ref[...], shift_ref[...], low_at, up_at, time_at, samples)

    pending = []
    for piece in turns:
        arrived = got.at[pl.ds(0, count - 1), pl.ds(0, piece_rows)]
        pltpu.make_async_copy(arrived, arrived, recv_sem.at[piece]).wait()
        for step in range(local, levels):
            part = (2 << step) // pieces
            places = places_of(step, 0, bands, piece * part, (piece + 1) * part)
            out = states[step - local]

            def read(row):
                if step == local:
                    return got[row // rows_each, pl.ds(row % rows_each, ROWS)]
                return states[step - local - 1][pl.ds(row, ROWS)]

            share = -(-len(pending) // (levels - step))
            for run in pending[:share]:
                run()
            pending = pending[share:]
            for at in range(0, len(places), BATCH):
                batch = places[at : at + BATCH]
                rows = [pl.ds(row, ROWS) for row, _, _, _ in batch]
                values = merge(
                    [read(row) for _, _, row, _ in batch],
                    [read(row) for _, _, _, row in batch],
                    [low_at[step - local, row] for row in rows],
                    [up_at[step - local, row] for row in rows],
                    [time_at[step - local, row] for row in rows],
                    samples,
                )
                for row, value in zip(rows, values):
                    out[row] = value
        size = bands // pieces
        pending = scores(states[-1], piece * size, size, boxes_ref, limit_ref, out_ref)
    for run in pending:
        run()
    sent = ready.at[pl.ds(0, count - 1)]
    pltpu.make_async_copy(sent, sent, send_sem).wait()


def shards(intensities, lower_index, upper_index, delay_shift, widths, max_delay):
    beam_count = lax.axis_size("beam")
    chan_count = lax.axis_size("chan")
    count = beam_count * chan_count
    beams, channels, samples = intensities.shape
    rows_each = channels // SUB0
    bands = count * rows_each
    levels = lower_index.shape[0]
    local = rows_each.bit_length() - 1
    pieces = rows_each // ROWS
    return pl.pallas_call(
        functools.partial(kernel, beam_count, chan_count, levels, pieces),
        out_shape=pltpu.VMEM((1, widths.shape[0], bands), jnp.float32),
        in_specs=[pl.BlockSpec(memory_space=pltpu.HBM)] * 6,
        out_specs=pl.BlockSpec(memory_space=pltpu.VMEM),
        scratch_shapes=[
            pltpu.VMEM((beams, channels, samples), intensities.dtype),
            pltpu.VMEM(lower_index.shape, jnp.int32),
            pltpu.VMEM(upper_index.shape, jnp.int32),
            pltpu.VMEM(delay_shift.shape, jnp.int32),
            pltpu.SMEM(widths.shape, jnp.int32),
            pltpu.SMEM(max_delay.shape, jnp.int32),
            pltpu.VMEM((widths.shape[0], samples, 2 * samples), jnp.bfloat16),
            pltpu.VMEM((max(1, local - 3), count, rows_each, samples), jnp.float32),
            pltpu.VMEM((count, rows_each, samples), jnp.float32),
            pltpu.VMEM((count, rows_each, samples), jnp.float32),
        ]
        + [pltpu.VMEM((bands, samples), jnp.float32)] * (levels - local)
        + [pltpu.VMEM((local, rows_each, samples), jnp.int32)] * 3
        + [pltpu.VMEM((levels - local, bands, samples), jnp.int32)] * 3
        + [
            pltpu.SemaphoreType.DMA((chan_count // 2, beam_count)),
            pltpu.SemaphoreType.DMA((5,)),
            pltpu.SemaphoreType.DMA,
            pltpu.SemaphoreType.DMA((pieces,)),
        ],
        compiler_params=pltpu.CompilerParams(
            collective_id=0, has_side_effects=True, vmem_limit_bytes=56 * 1024 * 1024
        ),
        name="search",
    )(intensities, lower_index, upper_index, delay_shift, widths, max_delay)


def solution(mesh):
    in_specs = (P(None, ("beam", "chan"), None), P(), P(), P(), P(), P(("beam", "chan")))
    out_specs = P(("beam", "chan"), None, None)
    return jax.shard_map(shards, mesh=mesh, in_specs=in_specs, out_specs=out_specs, check_vma=False)
```

```python
import functools

import jax
import jax.numpy as jnp
from jax import lax
from jax.experimental import pallas as pl
from jax.experimental.pallas import tpu as pltpu
from jax.sharding import PartitionSpec as P

SUB0 = 8
ROWS = 8
BATCH = 32
MESH = pl.DeviceIdType.MESH


def take(values, index, axis):
    return jnp.take_along_axis(values, index, axis=axis, mode="promise_in_bounds")


def source_base(trial, width):
    half = width // 2
    return jnp.minimum(4 * (trial // ROWS), jnp.maximum(half - ROWS, 0))


def build_indices(steps, lower, upper, shift, low_at, up_at, time_at, samples):
    levels, bands = lower.shape
    kept = low_at.shape[1]
    depth = 16
    zeros = jnp.zeros((depth - levels, bands), jnp.int32)
    lower = jnp.concatenate([lower, zeros], axis=0)
    upper = jnp.concatenate([upper, zeros], axis=0)
    shift = jnp.concatenate([shift, zeros], axis=0)
    level = lax.broadcasted_iota(jnp.int32, (depth, bands), 0)
    row = lax.broadcasted_iota(jnp.int32, (depth, bands), 1)
    width = jnp.left_shift(jnp.int32(2), level)
    trial = row & (width - 1)
    inside = (row & (ROWS - 1)) - trial
    skip = source_base(trial, width)
    lower = jnp.where(level <= 2, inside + lower, lower - skip) & (ROWS - 1)
    upper = jnp.where(level <= 2, inside + width // 2 + upper, upper - skip) & (ROWS - 1)
    packed = jnp.concatenate(
        [(lower + ROWS * upper).astype(jnp.float32), jnp.minimum(shift, samples).astype(jnp.float32)],
        axis=0,
    ).astype(jnp.bfloat16)
    entry = lax.broadcasted_iota(jnp.int32, (2 * depth, samples), 0)
    time = lax.broadcasted_iota(jnp.int32, (kept, samples), 1)
    for at, step in enumerate(steps):
        spread = jnp.where(entry == step, 256.0, jnp.where(entry == depth + step, 1.0, 0.0))
        value = lax.dot_general(
            packed,
            spread.astype(jnp.bfloat16),
            (((0,), (0,)), ((), ())),
            preferred_element_type=jnp.float32,
        )[:kept].astype(jnp.int32)
        low_at[at] = (value >> 8) & (ROWS - 1)
        up_at[at] = value >> 11
        time_at[at] = time - (value & 255)


def merge(lowers, uppers, lows, ups, whens, samples):
    uppers = [take(v, up, 0) for v, up in zip(uppers, ups)]
    lowers = [take(v, low, 0) for v, low in zip(lowers, lows)]
    uppers = [take(v, when & (samples - 1), 1) for v, when in zip(uppers, whens)]
    return [v + jnp.where(when >= 0, u, 0.0) for v, u, when in zip(lowers, uppers, whens)]


def places_of(step, start, size, first, last):
    width = 2 << step
    places = []
    for base in range(0, size, width):
        for trial in range(first, last, ROWS):
            skip = min(4 * (trial // ROWS), max(width // 2 - ROWS, 0))
            places.append((base + trial, start + base + trial, start + base + skip, start + base + width // 2 + skip))
    return places


def build_boxes(widths_ref, boxes_ref):
    boxes, samples, _ = boxes_ref.shape
    source = lax.broadcasted_iota(jnp.int32, (samples, samples), 1)
    target = lax.broadcasted_iota(jnp.int32, (samples, samples), 0)
    back = target - source
    for box in range(boxes):
        width = widths_ref[box]
        hit = jnp.where((back >= 0) & (back < width), 1.0, 0.0)
        mean = jnp.minimum(width, samples - source).astype(jnp.float32) * (1.0 / samples)
        value = (hit - mean).astype(jnp.bfloat16)
        boxes_ref[box, :, pl.ds(0, samples)] = value
        boxes_ref[box, :, pl.ds(samples, samples)] = value


def scores(trials_ref, start, size, boxes_ref, limit_ref, out_ref):
    boxes, samples, _ = boxes_ref.shape
    chunk = min(256, size)
    steps = []

    def add(at):
        both, tops, spreads = [], [], []

        def split():
            trials = trials_ref[pl.ds(at, chunk)]
            high = trials.astype(jnp.bfloat16)
            low = (trials - high.astype(jnp.float32)).astype(jnp.bfloat16)
            both.append(jnp.concatenate([high, low], axis=1))

        def one(box):
            offset = lax.dot_general(
                boxes_ref[box], both[0], (((1,), (1,)), ((), ())), preferred_element_type=jnp.float32
            )
            tops.append(jnp.max(offset, axis=0, keepdims=True))
            spreads.append(jnp.sum(offset * offset, axis=0, keepdims=True))

        def finish():
            top = jnp.concatenate(tops, axis=0)
            spread = jnp.concatenate(spreads, axis=0) * (1.0 / samples)
            keep = lax.broadcasted_iota(jnp.int32, (boxes, chunk), 1) + at <= limit_ref[0]
            out_ref[0, :, pl.ds(at, chunk)] = jnp.where(keep, top / jnp.sqrt(spread + 1e-05), 0.0)

        steps.extend([split] + [functools.partial(one, box) for box in range(boxes)] + [finish])

    for at in range(start, start + size, chunk):
        add(at)
    return steps


def schedule(groups, near, turns):
    cut = max(1, len(turns) // 2)
    later = [at for at in range(1, groups) if at not in near]
    items = [(0, 0)] + [(0, piece, 0) for piece in turns] + [(0, 1)] + [(0, piece, 1) for piece in turns[:cut]]
    for at in later:
        items += [(at, 2), (at, turns[0], 0), (at, turns[0], 1)] + [(at, piece, 0) for piece in turns[1:2]]
    for at in near:
        items += [(at, 2)] + [(at, piece, 2) for piece in turns[:cut]]
    for turn in range(1, len(turns)):
        ahead = turns[turn + cut - 1 : turn + cut]
        items += [(0, piece, 1) for piece in ahead]
        for at in later:
            items += [(at, turns[turn], 1)] + [(at, piece, 0) for piece in turns[turn + 1 : turn + 2]]
        items += [(at, piece, 2) for at in near for piece in ahead]
    return items


def kernel(
    beam_count, chan_count, levels, pieces,
    x_hbm, lower_hbm, upper_hbm, shift_hbm, widths_hbm, limit_hbm, out_ref,
    x_ref, lower_ref, upper_ref, shift_ref, widths_ref, limit_ref, boxes_ref, work, ready, got, *rest,
):
    count = beam_count * chan_count
    channels, samples = x_ref.shape[1], x_ref.shape[2]
    rows_each = channels // SUB0
    bands = count * rows_each
    local = rows_each.bit_length() - 1
    states, rest = rest[: levels - local], rest[levels - local :]
    low_in, up_in, time_in, low_at, up_at, time_at, load_sem, table_sem, send_sem, recv_sem = rest
    beam, chan = lax.axis_index("beam"), lax.axis_index("chan")
    me = beam * chan_count + chan
    piece_rows = rows_each // pieces

    pair, core = chan // 2, chan % 2
    half = chan_count // 4
    side = pair // half
    far = [(1 - side) * half + at for at in range(half)]
    near = [side * half + (pair + 1 + at) % half for at in range(half)]
    beam_steps = [(1 << bit) * (1 - 2 * (beam // (1 << bit) % 2)) for bit in range(beam_count.bit_length() - 1)]

    def other_beam(mask):
        value = beam
        for bit, step in enumerate(beam_steps):
            if mask >> bit & 1:
                value = value + step
        return value

    def group(pair_to, beams, lead):
        return [(at, pair_to * 2 + (lead + turn) % 2) for at in beams for turn in range(2)]

    fixed = [jnp.int32(at) for at in range(beam_count)]
    turned = [other_beam(mask) for mask in range(beam_count)]
    order = [(far[0], group(far[0], fixed, 1))]
    order += [(pair_to, group(pair_to, turned, core)) for pair_to in near]
    order += [(pair_to, group(pair_to, fixed, 1)) for pair_to in far[1:]]
    own = half

    barrier = pltpu.get_barrier_semaphore()
    loads = []
    for at, (pair_to, devices) in enumerate(order):
        loads.append([])
        for place in range(0, len(devices), 2):
            rows = pl.ds(devices[place][0] * chan_count + pair_to * 2, 2)
            loads[-1].append(pltpu.make_async_copy(x_hbm.at[rows], x_ref.at[rows], load_sem.at[at, place // 2]))
    others = [(lower_hbm, lower_ref), (upper_hbm, upper_ref), (shift_hbm, shift_ref), (widths_hbm, widths_ref), (limit_hbm, limit_ref)]
    tables = [pltpu.make_async_copy(source, target, table_sem.at[at]) for at, (source, target) in enumerate(others)]
    for table in tables:
        table.start()
    for load in loads[0]:
        load.start()
    for at, (_, devices) in enumerate(order):
        for place, device in enumerate(devices):
            if (at, place) != (own, 0):
                pl.semaphore_signal(barrier, inc=1, device_id=device, device_id_type=MESH)
    for group_loads in loads[1:]:
        for load in group_loads:
            load.start()

    band = lax.broadcasted_iota(jnp.int32, (rows_each, channels), 0)
    channel = lax.broadcasted_iota(jnp.int32, (rows_each, channels), 1)
    adder = jnp.where(channel // SUB0 == band, 1.0, 0.0).astype(jnp.bfloat16)
    for table in tables:
        table.wait()
    block = 128
    first = me * rows_each
    lanes = pl.ds(pl.multiple_of(first // block * block, block), block)
    away = (block - first % block) % block
    mine = [pltpu.roll(ref[:, lanes], away, 1) for ref in (lower_ref, upper_ref, shift_ref)]
    build_indices(range(local), *mine, low_in, up_in, time_in, samples)

    def dedisperse(beams):
        sums = []
        for at in range(0, len(beams), 2):
            both = jnp.concatenate([x_ref[beam_at] for beam_at in beams[at : at + 2]], axis=1)
            both = jnp.dot(adder, both, preferred_element_type=jnp.float32)
            sums += [both[:, lane : lane + samples] for lane in range(0, both.shape[1], samples)]
        tiles = [(at, row) for at in beams for row in range(0, rows_each, ROWS)]
        values = [v[row : row + ROWS] for v in sums for row in range(0, rows_each, ROWS)]
        for step in range(local):
            lows = [low_in[step, pl.ds(row, ROWS)] for _, row in tiles]
            ups = [up_in[step, pl.ds(row, ROWS)] for _, row in tiles]
            whens = [time_in[step, pl.ds(row, ROWS)] for _, row in tiles]
            if step < 3:
                lowers = uppers = values
            else:
                places = places_of(step, 0, rows_each, 0, 2 << step)
                lowers = [work[step - 3, at, pl.ds(row, ROWS)] for at in beams for _, _, row, _ in places]
                uppers = [work[step - 3, at, pl.ds(row, ROWS)] for at in beams for _, _, _, row in places]
            values = merge(lowers, uppers, lows, ups, whens, samples)
            if step >= 2:
                for (at, row), value in zip(tiles, values):
                    if step < local - 1:
                        work[step - 2, at, pl.ds(row, ROWS)] = value
                    else:
                        ready[at, pl.ds(row, ROWS)] = value

    def send(at, place, piece):
        device = order[at][1][place]
        rows = pl.ds(piece * piece_rows, piece_rows)
        pltpu.make_async_remote_copy(
            src_ref=ready.at[device[0] * chan_count + device[1], rows],
            dst_ref=got.at[me, rows],
            send_sem=send_sem,
            recv_sem=recv_sem.at[piece],
            device_id=device,
            device_id_type=MESH,
        ).start()

    def compute(at, part):
        for mask in sorted({place // 2 for place in parts[part]}):
            loads[at][mask].wait()
        beams = [device[0] * chan_count + device[1] for device in order[at][1]]
        for first in range(parts[part].start, parts[part].stop, per):
            dedisperse(beams[first : min(first + per, parts[part].stop)])

    parts = (range(2), range(2, 2 * beam_count), range(2 * beam_count))
    per = max(1, BATCH * ROWS // rows_each)
    turns = list(reversed(range(pieces)))
    greeted = False
    for item in schedule(len(order), range(1, half + 1), turns):
        if len(item) == 2:
            compute(*item)
            continue
        if not greeted:
            pl.semaphore_wait(barrier, count - 1)
            greeted = True
        at, piece, part = item
        for to in parts[part]:
            if (at, to) != (own, 0):
                send(at, to, piece)
    got[me] = ready[me]
    build_boxes(widths_ref, boxes_ref)
    build_indices(range(local, levels), lower_ref[...], upper_ref[...], shift_ref[...], low_at, up_at, time_at, samples)

    pending = []
    for piece in turns:
        arrived = got.at[pl.ds(0, count - 1), pl.ds(0, piece_rows)]
        pltpu.make_async_copy(arrived, arrived, recv_sem.at[piece]).wait()
        for step in range(local, levels):
            part = (2 << step) // pieces
            places = places_of(step, 0, bands, piece * part, (piece + 1) * part)
            out = states[step - local]

            def read(row):
                if step == local:
                    return got[row // rows_each, pl.ds(row % rows_each, ROWS)]
                return states[step - local - 1][pl.ds(row, ROWS)]

            share = -(-len(pending) // (levels - step))
            for run in pending[:share]:
                run()
            pending = pending[share:]
            for at in range(0, len(places), BATCH):
                batch = places[at : at + BATCH]
                rows = [pl.ds(row, ROWS) for row, _, _, _ in batch]
                values = merge(
                    [read(row) for _, _, row, _ in batch],
                    [read(row) for _, _, _, row in batch],
                    [low_at[step - local, row] for row in rows],
                    [up_at[step - local, row] for row in rows],
                    [time_at[step - local, row] for row in rows],
                    samples,
                )
                for row, value in zip(rows, values):
                    out[row] = value
        size = bands // pieces
        pending = scores(states[-1], piece * size, size, boxes_ref, limit_ref, out_ref)
    for run in pending:
        run()
    sent = ready.at[pl.ds(0, count - 1)]
    pltpu.make_async_copy(sent, sent, send_sem).wait()


def shards(intensities, lower_index, upper_index, delay_shift, widths, max_delay):
    beam_count = lax.axis_size("beam")
    chan_count = lax.axis_size("chan")
    count = beam_count * chan_count
    beams, channels, samples = intensities.shape
    rows_each = channels // SUB0
    bands = count * rows_each
    levels = lower_index.shape[0]
    local = rows_each.bit_length() - 1
    pieces = rows_each // ROWS
    return pl.pallas_call(
        functools.partial(kernel, beam_count, chan_count, levels, pieces),
        out_shape=pltpu.VMEM((1, widths.shape[0], bands), jnp.float32),
        in_specs=[pl.BlockSpec(memory_space=pltpu.HBM)] * 6,
        out_specs=pl.BlockSpec(memory_space=pltpu.VMEM),
        scratch_shapes=[
            pltpu.VMEM((beams, channels, samples), intensities.dtype),
            pltpu.VMEM(lower_index.shape, jnp.int32),
            pltpu.VMEM(upper_index.shape, jnp.int32),
            pltpu.VMEM(delay_shift.shape, jnp.int32),
            pltpu.SMEM(widths.shape, jnp.int32),
            pltpu.SMEM(max_delay.shape, jnp.int32),
            pltpu.VMEM((widths.shape[0], samples, 2 * samples), jnp.bfloat16),
            pltpu.VMEM((max(1, local - 3), count, rows_each, samples), jnp.float32),
            pltpu.VMEM((count, rows_each, samples), jnp.float32),
            pltpu.VMEM((count, rows_each, samples), jnp.float32),
        ]
        + [pltpu.VMEM((bands, samples), jnp.float32)] * (levels - local)
        + [pltpu.VMEM((local, rows_each, samples), jnp.int32)] * 3
        + [pltpu.VMEM((levels - local, bands, samples), jnp.int32)] * 3
        + [
            pltpu.SemaphoreType.DMA((chan_count // 2, beam_count)),
            pltpu.SemaphoreType.DMA((5,)),
            pltpu.SemaphoreType.DMA,
            pltpu.SemaphoreType.DMA((pieces,)),
        ],
        compiler_params=pltpu.CompilerParams(
            collective_id=0, has_side_effects=True, vmem_limit_bytes=56 * 1024 * 1024
        ),
        name="search",
    )(intensities, lower_index, upper_index, delay_shift, widths, max_delay)


def solution(mesh):
    in_specs = (P(None, ("beam", "chan"), None), P(), P(), P(), P(), P(("beam", "chan")))
    out_specs = P(("beam", "chan"), None, None)
    return jax.shard_map(shards, mesh=mesh, in_specs=in_specs, out_specs=out_specs, check_vma=False)
```
